32 devices in a mesh: dp: 2 (over x), seq: 2 (over y), tensor: 8 (over z, core).
Axes of the slice: x: 2, y: 2, z: 4, core: 2. Of those that a mesh axis runs over, the one named last changes fastest.
Arguments:
- activations: bfloat16 [4, 384, 28672], P('dp', 'seq', 'tensor'), may hold values from -6 to 6
- gradients: bfloat16 [4, 384, 8192], P('dp', 'seq', 'tensor'), may hold values from -6 to 6
- basis_in: bfloat16 [28672, 128], P('tensor', 'seq'), may hold values from -0.03125 to 0.03125
- basis_out: bfloat16 [8192, 768], P('tensor', 'seq'), may hold values from -0.0625 to 0.0625
Outputs:
- corrected: float32 [128, 768], P(('seq', 'tensor'))
The draws below stay inside these ranges and needn't reach their ends.
All inputs are finite; a program needn't handle non-finite values.
Results may differ from the reference program's by a relative error of at most 0.0034.
Values may be sent and summed in bfloat16 or wider, within the bound.
A program may use at most 64 MiB of HBM per device.

```python
import jax
import jax.numpy as jnp

A = 28672
G = 8192
KG = 768
SEQS = 4
LEN = 384
KA = 128


def shard_levels(own_key, extent, split, low, high):
    gain, own = 1.0, jax.random.fold_in(own_key, 6)
    for position, parts in split:
        draws = jnp.exp(jax.random.uniform(jax.random.fold_in(own, position), (parts,), jnp.float32, low / len(split), high / len(split)))
        gain = gain * jnp.repeat(draws, extent[position] // parts).reshape([-1 if axis == position else 1 for axis in range(len(extent))])
    return gain


def normal_values(rng, extent, width, most, cuts=(), kind=jnp.bfloat16):
    drawn = width * jax.random.normal(rng, extent, jnp.float32)
    if cuts:
        drawn = drawn * shard_levels(rng, extent, cuts, -0.22, 0.18)
    return jnp.clip(drawn, -most, most).astype(kind)


def setup_inputs(seed: int = 0) -> dict:
    keys = jax.random.split(jax.random.key(seed), 5)
    return {
        "activations": normal_values(keys[0], (SEQS, LEN, A), 1.0, 6.0, ((0, 2), (1, 2), (2, 8))),
        "gradients": normal_values(keys[1], (SEQS, LEN, G), 1.0, 6.0, ((0, 2), (1, 2), (2, 8))),
        "basis_in": normal_values(keys[2], (A, KA), A ** -0.5, 0.03125, ((0, 8), (1, 2))),
        "basis_out": normal_values(keys[3], (G, KG), G ** -0.5, 0.0625, ((0, 8), (1, 2))),
    }


def reference(activations, gradients, basis_in, basis_out):
    act_rows = activations.reshape(SEQS * LEN, A)
    grad_rows = gradients.reshape(SEQS * LEN, G)
    projected_act = jnp.dot(act_rows, basis_in, preferred_element_type=jnp.float32).astype(jnp.bfloat16)
    projected_grad = jnp.dot(grad_rows, basis_out, preferred_element_type=jnp.float32).astype(jnp.bfloat16)
    projected_act = projected_act.reshape(SEQS, LEN, KA).astype(jnp.float32)
    projected_grad = projected_grad.reshape(SEQS, LEN, KG).astype(jnp.float32)
    blocks = jnp.einsum("stk,stj->skj", projected_act, projected_grad)
    corrected = jnp.sum(blocks * blocks, axis=0) / (SEQS * LEN)
    return corrected
```

```python
import functools

import jax
import jax.numpy as jnp
from jax import lax
from jax.experimental import pallas as pl
from jax.experimental.pallas import tpu as pltpu
from jax.sharding import PartitionSpec as P

MESH = pl.DeviceIdType.MESH
F32 = jnp.float32
BF16 = jnp.bfloat16
CHUNKS = 2


def kernel(
    dims,
    act_hbm, grad_hbm, pin_hbm, bout_hbm, out_ref,
    act, grad, pin_own, pin_oth, bout_own, bout_oth,
    gpart, gmate, gown, gsend, grecv,
    apart, arecv, afull,
    bpart, brecv, spad, strans, frecv,
    local_sem, ysend, yrecv, xsend, xrecv, msend, mrecv, zsend, zrecv,
    a1send, a1recv, a2send, a2recv, bsend, brecv_sem, fsend, frecv_sem,
):
    dps, seqs, tensors, nz, cols, count = dims
    dp = lax.axis_index("dp")
    y = lax.axis_index("seq")
    t = lax.axis_index("tensor")
    z = t // 2
    c = lax.rem(t, 2)
    oy = 1 - y
    odp = 1 - dp
    mate = z * 2 + (1 - c)
    tokens = grad.shape[0]
    per_seq = tokens // 2

    def remote(src, dst, s, r, to):
        copy = pltpu.make_async_remote_copy(
            src_ref=src, dst_ref=dst, send_sem=s, recv_sem=r,
            device_id=to, device_id_type=MESH,
        )
        copy.start()
        return copy

    loads = []
    for n, (src, dst) in enumerate(
        ((bout_hbm, bout_own), (grad_hbm, grad), (pin_hbm, pin_own), (act_hbm, act))
    ):
        copy = pltpu.make_async_copy(src, dst, local_sem.at[n])
        copy.start()
        loads.append(copy)

    barrier = pltpu.get_barrier_semaphore()
    for ddp in range(dps):
        for d in range(tensors):
            if ddp + d == 0:
                continue
            pl.semaphore_signal(
                barrier, inc=1,
                device_id=(lax.rem(dp + ddp, dps), y, lax.rem(t + d, tensors)),
                device_id_type=MESH,
            )
    pl.semaphore_signal(barrier, inc=1, device_id=(dp, oy, t), device_id_type=MESH)
    pl.semaphore_wait(barrier, dps * tensors)

    def rows(ref, half, chunk):
        size = ref.shape[0] // (2 * CHUNKS)
        return pl.ds(pl.multiple_of((half * CHUNKS + chunk) * size, size), size)

    sends = []
    ycopies = []
    for n, (src, dst) in enumerate(((pin_hbm, pin_oth), (bout_hbm, bout_oth))):
        for k in range(CHUNKS):
            i = n * CHUNKS + k
            part = rows(dst, dp, k)
            ycopies.append(
                remote(src.at[part], dst.at[part], ysend.at[i], yrecv.at[i], (dp, oy, t))
            )
    sends += ycopies
    xcopies = []

    def forward(n, dst):
        for k in range(CHUNKS):
            i = n * CHUNKS + k
            ycopies[i].wait_recv()
            part = rows(dst, dp, k)
            xcopies.append(
                remote(dst.at[part], dst.at[part], xsend.at[i], xrecv.at[i], (odp, y, t))
            )

    def project_grad(basis, h, slot):
        total = lax.dot_general(
            basis[...], grad[...], (((0,), (1,)), ((), ())), preferred_element_type=F32
        )
        gpart[slot] = total.reshape(2, nz, cols, tokens)
        return remote(
            gpart.at[slot, 1 - c], gmate.at[h], msend.at[slot], mrecv.at[slot],
            (dp, y, mate),
        )

    def scatter_grad(copy, h, slot):
        copy.wait_recv()
        pair = gpart[slot, c] + gmate[h]
        gsend[slot] = pair.astype(BF16)
        gown[slot] = gpart[slot, c, z] + gmate[h, z]
        copies = []
        for d in range(1, nz):
            oz = lax.rem(z + d, nz)
            i = slot * (nz - 1) + d - 1
            copies.append(
                remote(
                    gsend.at[slot, oz], grecv.at[slot, d - 1], zsend.at[i], zrecv.at[i],
                    (dp, y, oz * 2 + c),
                )
            )
        return copies

    loads[0].wait()
    loads[1].wait()
    mate0 = project_grad(bout_own, 0, 0)
    forward(0, pin_oth)
    loads[2].wait()
    loads[3].wait()
    half = pin_own.shape[0]
    left_own = jnp.dot(act[:, :half], pin_own[...], preferred_element_type=F32)
    right_own = jnp.dot(act[:, half:], pin_own[...], preferred_element_type=F32)
    z0 = scatter_grad(mate0, 0, 0)

    for k in range(CHUNKS):
        xcopies[k].wait_recv()
    left_oth = jnp.dot(act[:, :half], pin_oth[...], preferred_element_type=F32)
    right_oth = jnp.dot(act[:, half:], pin_oth[...], preferred_element_type=F32)
    kk = pin_own.shape[1]
    lane = lax.broadcasted_iota(jnp.int32, (tokens, kk), 1)
    low = lane < kk // 2
    own = jnp.where(low, left_own, 0.0) + pltpu.roll(jnp.where(low, 0.0, right_own), kk // 2, 1)
    oth = jnp.where(low, left_oth, 0.0) + pltpu.roll(jnp.where(low, 0.0, right_oth), kk // 2, 1)
    first = jnp.where(y == 0, own, oth)
    second = jnp.where(y == 0, oth, own)
    apart[...] = (first + pltpu.roll(second, kk // 2, 1)).reshape(apart.shape)
    a1 = []
    for d in range(1, tensors):
        ot = lax.rem(t + d, tensors)
        a1.append(
            remote(apart.at[ot], arecv.at[d - 1], a1send.at[d - 1], a1recv.at[d - 1], (dp, y, ot))
        )

    forward(1, bout_oth)
    total = apart[t]
    for d in range(1, tensors):
        a1[d - 1].wait_recv()
        total = total + arecv[d - 1]
    afull[t] = total.astype(BF16)
    a2 = []
    for d in range(1, tensors):
        ot = lax.rem(t + d, tensors)
        a2.append(
            remote(afull.at[t], afull.at[t], a2send.at[d - 1], a2recv.at[d - 1], (dp, y, ot))
        )

    for k in range(CHUNKS):
        xcopies[CHUNKS + k].wait_recv()
    mate1 = project_grad(bout_oth, 1, 1)
    for copy in a2:
        copy.wait_recv()
    whole = afull[...].astype(F32).reshape(tokens, kk)
    turned = pltpu.roll(whole, kk // 2, 1)
    row = lax.broadcasted_iota(jnp.int32, (tokens, kk), 0)
    mine = (row < per_seq) == low
    masked0 = jnp.where(mine, jnp.where(low, whole, turned), 0.0).astype(BF16)
    masked1 = jnp.where(mine, jnp.where(low, turned, whole), 0.0).astype(BF16)
    z1 = scatter_grad(mate1, 1, 1)

    def finish_grad(slot, copies):
        total = gown[slot]
        for d in range(1, nz):
            copies[d - 1].wait_recv()
            total = total + grecv[slot, d - 1].astype(F32)
        return total.astype(BF16)

    def outer(part, slot):
        at = jnp.where(y == slot, 0, 1)
        bpart[0, at] = jnp.dot(part, masked0, preferred_element_type=F32)
        bpart[1, at] = jnp.dot(part, masked1, preferred_element_type=F32)

    outer(finish_grad(0, z0), 0)
    outer(finish_grad(1, z1), 1)
    bcopy = remote(bpart.at[oy], brecv, bsend.at[0], brecv_sem.at[0], (dp, oy, t))
    spad[...] = jnp.zeros_like(spad)
    bcopy.wait_recv()
    both = (bpart[y] + brecv[...]).reshape(2 * cols, kk)
    square = both * both
    spad[pl.ds(0, 2 * cols), :] = square + pltpu.roll(square, kk // 2, 1)
    strans[...] = spad[...].T.reshape(strans.shape)
    place = c * nz + z
    frecv[0, place] = strans[t]
    fcopies = []
    for ddp in range(dps):
        for d in range(tensors):
            if ddp + d == 0:
                continue
            i = ddp * tensors + d - 1
            ot = lax.rem(t + d, tensors)
            fcopies.append(
                remote(
                    strans.at[ot], frecv.at[ddp, place], fsend.at[i], frecv_sem.at[i],
                    (lax.rem(dp + ddp, dps), y, ot),
                )
            )
    for copy in fcopies:
        copy.wait_recv()
    out_ref[...] = (frecv[0] + frecv[1]) / count
    for copy in sends + xcopies + [mate0, mate1] + z0 + z1 + a1 + a2 + [bcopy] + fcopies:
        copy.wait_send()


def fused(activations, gradients, basis_in, basis_out):
    dps, seqs, tensors = lax.axis_size("dp"), lax.axis_size("seq"), lax.axis_size("tensor")
    s, length, width = activations.shape
    gwidth = gradients.shape[2]
    tokens = s * length
    nz = tensors // 2
    khalf = basis_in.shape[1]
    jhalf = basis_out.shape[1]
    kk = 2 * khalf
    cols = jhalf // tensors
    per = khalf // tensors
    count = s * dps * length * seqs
    packed = jnp.concatenate([basis_in[: width // 2], basis_in[width // 2 :]], axis=1)
    dma = pltpu.SemaphoreType.DMA
    tok_own = tokens // tensors
    out = pl.pallas_call(
        functools.partial(kernel, (dps, seqs, tensors, nz, cols, count)),
        out_shape=jax.ShapeDtypeStruct((tensors, per, 128), F32),
        in_specs=[pl.BlockSpec(memory_space=pl.ANY)] * 4,
        out_specs=pl.BlockSpec(memory_space=pltpu.VMEM),
        scratch_shapes=[
            pltpu.VMEM((tokens, width), BF16),
            pltpu.VMEM((tokens, gwidth), BF16),
            pltpu.VMEM((width // 2, kk), BF16),
            pltpu.VMEM((width // 2, kk), BF16),
            pltpu.VMEM((gwidth, jhalf), BF16),
            pltpu.VMEM((gwidth, jhalf), BF16),
            pltpu.VMEM((2, 2, nz, cols, tokens), F32),
            pltpu.VMEM((2, nz, cols, tokens), F32),
            pltpu.VMEM((2, cols, tokens), F32),
            pltpu.VMEM((2, nz, cols, tokens), BF16),
            pltpu.VMEM((2, nz - 1, cols, tokens), BF16),
            pltpu.VMEM((tensors, tok_own, kk), F32),
            pltpu.VMEM((tensors - 1, tok_own, kk), F32),
            pltpu.VMEM((tensors, tok_own, kk), BF16),
            pltpu.VMEM((2, 2, cols, kk), F32),
            pltpu.VMEM((2, cols, kk), F32),
            pltpu.VMEM((128, kk), F32),
            pltpu.VMEM((kk // per, per, 128), F32),
            pltpu.VMEM((dps, tensors, per, 128), F32),
            dma((4,)),
            dma((2 * CHUNKS,)), dma((2 * CHUNKS,)),
            dma((2 * CHUNKS,)), dma((2 * CHUNKS,)),
            dma((2,)), dma((2,)),
            dma((2 * (nz - 1),)), dma((2 * (nz - 1),)),
            dma((tensors - 1,)), dma((tensors - 1,)),
            dma((tensors - 1,)), dma((tensors - 1,)),
            dma((1,)), dma((1,)),
            dma((dps * tensors - 1,)), dma((dps * tensors - 1,)),
        ],
        compiler_params=pltpu.CompilerParams(
            collective_id=0, has_side_effects=True, vmem_limit_bytes=40 * 1024 * 1024
        ),
    )(
        activations.reshape(tokens, width),
        gradients.reshape(tokens, gwidth),
        packed,
        basis_out,
    )
    kept = out[:, :, : 2 * cols].reshape(tensors, per, 2, cols)
    return kept.transpose(1, 2, 0, 3).reshape(per, 2 * jhalf)


def general(activations, gradients, basis_in, basis_out):
    seq_count = lax.axis_size("seq")
    tensor_count = lax.axis_size("tensor")
    replica_count = lax.axis_size("dp")
    seqs_local = activations.shape[0]
    len_local = activations.shape[1]
    width_local = activations.shape[2]
    grad_partial = jnp.einsum(
        "sci,ij->scj",
        gradients,
        lax.all_gather(basis_out, "seq", axis=1, tiled=True),
        preferred_element_type=jnp.float32,
    )
    projected_grad = lax.psum(grad_partial, "tensor").astype(jnp.bfloat16)
    whole_basis = lax.all_gather(basis_in, "seq", axis=1, tiled=True)
    col_total = whole_basis.shape[1]
    per_device = col_total // (seq_count * tensor_count)
    arranged = whole_basis.reshape(width_local, seq_count, tensor_count, per_device)
    group_rows = seq_count * per_device
    product = jnp.einsum(
        "isTj,qci->Tsjqc", arranged, activations, preferred_element_type=jnp.float32
    )
    flat_act = lax.psum_scatter(
        product.reshape(group_rows * lax.axis_size("tensor"), seqs_local * len_local),
        "tensor",
        scatter_dimension=0,
        tiled=True,
    ).astype(jnp.bfloat16)
    projected_act = flat_act.reshape(flat_act.shape[0], seqs_local, len_local)
    partial_blocks = jnp.einsum(
        "rqc,qcj->qrj", projected_act, projected_grad, preferred_element_type=jnp.float32
    )
    blocks = lax.psum_scatter(partial_blocks, "seq", scatter_dimension=1, tiled=True)
    squared = jnp.sum(blocks * blocks, axis=0)
    summed = lax.psum(squared, "dp")
    return summed / (seqs_local * replica_count * len_local * seq_count)


def body(activations, gradients, basis_in, basis_out):
    dps, seqs, tensors = lax.axis_size("dp"), lax.axis_size("seq"), lax.axis_size("tensor")
    s, length, width = activations.shape
    tokens = s * length
    khalf, jhalf = basis_in.shape[1], basis_out.shape[1]
    fits = (
        dps == 2 and seqs == 2 and s == 2 and tensors % 2 == 0
        and khalf == 64 and khalf % (8 * tensors) == 0
        and tokens % (16 * tensors) == 0 and tokens % 128 == 0
        and jhalf % (16 * tensors) == 0 and 2 * jhalf // tensors <= 128
        and width % 256 == 0 and (width // 2) % (32 * CHUNKS) == 0
        and gradients.shape[2] % (32 * CHUNKS) == 0
        and tokens * width * 2 <= 8 * 1024 * 1024
    )
    return (fused if fits else general)(activations, gradients, basis_in, basis_out)


def solution(mesh):
    return jax.shard_map(
        body,
        mesh=mesh,
        in_specs=(
            P("dp", "seq", "tensor"),
            P("dp", "seq", "tensor"),
            P("tensor", "seq"),
            P("tensor", "seq"),
        ),
        out_specs=P(("seq", "tensor"), None),
        check_vma=False,
    )
```

```python
import functools

import jax
import jax.numpy as jnp
from jax import lax
from jax.experimental import pallas as pl
from jax.experimental.pallas import tpu as pltpu
from jax.sharding import PartitionSpec as P

MESH = pl.DeviceIdType.MESH
F32 = jnp.float32
BF16 = jnp.bfloat16
CHUNKS = 2


def kernel(
    dims,
    act_hbm, grad_hbm, pin_hbm, bout_hbm, out_ref,
    act, grad, pin, bout_own, bout_oth,
    gpart, gmate, gown, gsend, grecv, gfin,
    apart, arecv, afull,
    bpart, brecv, spad, strans, frecv,
    local_sem, ysend, yrecv, xsend, xrecv, msend, mrecv, zsend, zrecv,
    a1send, a1recv, a2send, a2recv, bsend, brecv_sem, fsend, frecv_sem,
):
    dps, seqs, tensors, nz, groups, cols, count = dims
    dp = lax.axis_index("dp")
    y = lax.axis_index("seq")
    t = lax.axis_index("tensor")
    z = t // 2
    c = lax.rem(t, 2)
    oy = 1 - y
    odp = 1 - dp
    mate = z * 2 + (1 - c)
    tokens, width = act.shape
    depth = grad.shape[1]
    per_seq = tokens // 2
    kk = afull.shape[2]

    def remote(src, dst, s, r, to):
        copy = pltpu.make_async_remote_copy(
            src_ref=src, dst_ref=dst, send_sem=s, recv_sem=r,
            device_id=to, device_id_type=MESH,
        )
        copy.start()
        return copy

    loads = []
    for n, (src, dst) in enumerate(
        ((bout_hbm, bout_own), (grad_hbm, grad), (pin_hbm, pin.at[y]), (act_hbm, act))
    ):
        copy = pltpu.make_async_copy(src, dst, local_sem.at[n])
        copy.start()
        loads.append(copy)

    barrier = pltpu.get_barrier_semaphore()
    for ddp in range(dps):
        for d in range(tensors):
            if ddp + d == 0:
                continue
            pl.semaphore_signal(
                barrier, inc=1,
                device_id=(lax.rem(dp + ddp, dps), y, lax.rem(t + d, tensors)),
                device_id_type=MESH,
            )
    pl.semaphore_signal(barrier, inc=1, device_id=(dp, oy, t), device_id_type=MESH)
    pl.semaphore_wait(barrier, dps * tensors)

    pieces = CHUNKS + groups

    def piece(i, own_in, in_slot, own_out):
        if i < CHUNKS:
            size = width // (2 * CHUNKS)
            at = pl.ds(pl.multiple_of((dp * CHUNKS + i) * size, 128), size)
            return own_in.at[:, at] if in_slot is None else own_in.at[in_slot, :, at]
        at = pl.ds(pl.multiple_of(dp * (depth // 2), 16), depth // 2)
        return own_out.at[at, pl.ds((i - CHUNKS) * 128, 128)]

    ycopies = []
    xcopies = []

    def send_y():
        i = len(ycopies)
        if i < pieces:
            ycopies.append(
                remote(
                    piece(i, pin_hbm, None, bout_hbm), piece(i, pin, y, bout_oth),
                    ysend.at[i], yrecv.at[i], (dp, oy, t),
                )
            )

    def forward():
        i = len(xcopies)
        ycopies[i].wait_recv()
        send_y()
        ref = piece(i, pin, oy, bout_oth)
        xcopies.append(remote(ref, ref, xsend.at[i], xrecv.at[i], (odp, y, t)))

    mates = []

    def project_grad(basis, first, number):
        n = len(mates)
        total = lax.dot_general(
            basis, grad[...], (((0,), (1,)), ((), ())), preferred_element_type=F32
        )
        gpart[first : first + number] = total.reshape(number, 2, nz, cols, tokens)
        part = pl.ds(first, number)
        mates.append(
            remote(
                gpart.at[part, 1 - c], gmate.at[part], msend.at[n], mrecv.at[n],
                (dp, y, mate),
            )
        )

    zcopies = []

    def scatter_grad(n, first, number):
        mates[n].wait_recv()
        part = pl.ds(first, number)
        gsend[part] = (gpart[part, c] + gmate[part]).astype(BF16)
        gown[part] = gpart[part, c, z] + gmate[part, z]
        copies = []
        for d in range(1, nz):
            oz = lax.rem(z + d, nz)
            i = n * (nz - 1) + d - 1
            copies.append(
                remote(
                    gsend.at[part, oz], grecv.at[d - 1, part], zsend.at[i], zrecv.at[i],
                    (dp, y, oz * 2 + c),
                )
            )
        zcopies.append(copies)

    def finish_grad(n, first, number):
        part = pl.ds(first, number)
        total = gown[part]
        for d in range(1, nz):
            zcopies[n][d - 1].wait_recv()
            total = total + grecv[d - 1, part].astype(F32)
        gfin[part] = total.astype(BF16)

    def project_act(half):
        at = pl.ds(pl.multiple_of(half * (width // 2), 128), width // 2)
        basis = pin[:, :, at].reshape(kk, width // 2)
        return lax.dot_general(
            act[:, at], basis, (((1,), (1,)), ((), ())), preferred_element_type=F32
        )

    def outer(slot, masked0, masked1):
        at = jnp.where(y == slot, 0, 1)
        part = gfin[slot * groups : (slot + 1) * groups].reshape(groups * cols, tokens)
        bpart[0, at] = jnp.dot(part, masked0, preferred_element_type=F32)
        bpart[1, at] = jnp.dot(part, masked1, preferred_element_type=F32)

    send_y()
    send_y()
    loads[0].wait()
    loads[1].wait()
    project_grad(bout_own[...], 0, groups)
    forward()
    loads[2].wait()
    loads[3].wait()
    forward()
    apart[...] = project_act(dp).reshape(apart.shape)
    scatter_grad(0, 0, groups)
    forward()
    for i in range(CHUNKS):
        xcopies[i].wait_recv()
    apart[...] = apart[...] + project_act(odp).reshape(apart.shape)
    a1 = []
    for d in range(1, tensors):
        ot = lax.rem(t + d, tensors)
        a1.append(
            remote(apart.at[ot], arecv.at[d - 1], a1send.at[d - 1], a1recv.at[d - 1], (dp, y, ot))
        )
    a2 = []
    for g in range(groups):
        if g + 1 < groups:
            forward()
        if g == 1:
            total = apart[t]
            for d in range(1, tensors):
                a1[d - 1].wait_recv()
                total = total + arecv[d - 1]
            afull[t] = total.astype(BF16)
            for d in range(1, tensors):
                ot = lax.rem(t + d, tensors)
                a2.append(
                    remote(
                        afull.at[t], afull.at[t], a2send.at[d - 1], a2recv.at[d - 1],
                        (dp, y, ot),
                    )
                )
        if g == groups - 1:
            finish_grad(0, 0, groups)
        xcopies[CHUNKS + g].wait_recv()
        project_grad(bout_oth[:, g * 128 : (g + 1) * 128], groups + g, 1)
        if g > 0:
            scatter_grad(g, groups + g - 1, 1)
    for copy in a2:
        copy.wait_recv()
    whole = afull[...].astype(F32).reshape(tokens, kk)
    turned = pltpu.roll(whole, kk // 2, 1)
    lane = lax.broadcasted_iota(jnp.int32, (tokens, kk), 1)
    row = lax.broadcasted_iota(jnp.int32, (tokens, kk), 0)
    low = lane < kk // 2
    mine = (row < per_seq) == low
    masked0 = jnp.where(mine, jnp.where(low, whole, turned), 0.0).astype(BF16)
    masked1 = jnp.where(mine, jnp.where(low, turned, whole), 0.0).astype(BF16)
    scatter_grad(groups, 2 * groups - 1, 1)
    outer(0, masked0, masked1)
    spad[...] = jnp.zeros_like(spad)
    for g in range(groups):
        finish_grad(1 + g, groups + g, 1)
    outer(1, masked0, masked1)
    bcopy = remote(bpart.at[oy], brecv, bsend.at[0], brecv_sem.at[0], (dp, oy, t))
    bcopy.wait_recv()
    both = (bpart[y] + brecv[...]).reshape(2 * groups * cols, kk)
    square = both * both
    spad[pl.ds(0, 2 * groups * cols), :] = square + pltpu.roll(square, kk // 2, 1)
    strans[...] = spad[...].T.reshape(strans.shape)
    place = c * nz + z
    frecv[0, place] = strans[t]
    fcopies = []
    for ddp in range(dps):
        for d in range(tensors):
            if ddp + d == 0:
                continue
            i = ddp * tensors + d - 1
            ot = lax.rem(t + d, tensors)
            fcopies.append(
                remote(
                    strans.at[ot], frecv.at[ddp, place], fsend.at[i], frecv_sem.at[i],
                    (lax.rem(dp + ddp, dps), y, ot),
                )
            )
    for copy in fcopies:
        copy.wait_recv()
    total = (frecv[0] + frecv[1]) / count
    lane = lax.broadcasted_iota(jnp.int32, total.shape[1:], 1)
    for block in range(2 * groups):
        found = jnp.zeros(total.shape[1:], F32)
        for p in range(tensors):
            shift = ((p - block) * cols) % 128
            moved = pltpu.roll(total[p], shift, 1) if shift else total[p]
            found = jnp.where(lane // cols == p, moved, found)
        out_ref[:, block * 128 : (block + 1) * 128] = found
    zall = [copy for copies in zcopies for copy in copies]
    for copy in ycopies + xcopies + mates + zall + a1 + a2 + [bcopy] + fcopies:
        copy.wait_send()


def fused(activations, gradients, basis_in, basis_out):
    dps, seqs, tensors = lax.axis_size("dp"), lax.axis_size("seq"), lax.axis_size("tensor")
    s, length, width = activations.shape
    gwidth = gradients.shape[2]
    tokens = s * length
    nz = tensors // 2
    khalf = basis_in.shape[1]
    jhalf = basis_out.shape[1]
    kk = 2 * khalf
    groups = jhalf // 128
    cols = 128 // tensors
    per = khalf // tensors
    count = s * dps * length * seqs
    dma = pltpu.SemaphoreType.DMA
    tok_own = tokens // tensors
    pieces = CHUNKS + groups
    shifts = (1 + groups) * (nz - 1)
    return pl.pallas_call(
        functools.partial(kernel, (dps, seqs, tensors, nz, groups, cols, count)),
        out_shape=jax.ShapeDtypeStruct((per, 2 * jhalf), F32),
        in_specs=[pl.BlockSpec(memory_space=pltpu.HBM)] * 4,
        out_specs=pl.BlockSpec(memory_space=pltpu.VMEM),
        scratch_shapes=[
            pltpu.VMEM((tokens, width), BF16),
            pltpu.VMEM((tokens, gwidth), BF16),
            pltpu.VMEM((2, khalf, width), BF16),
            pltpu.VMEM((gwidth, jhalf), BF16),
            pltpu.VMEM((gwidth, jhalf), BF16),
            pltpu.VMEM((2 * groups, 2, nz, cols, tokens), F32),
            pltpu.VMEM((2 * groups, nz, cols, tokens), F32),
            pltpu.VMEM((2 * groups, cols, tokens), F32),
            pltpu.VMEM((2 * groups, nz, cols, tokens), BF16),
            pltpu.VMEM((nz - 1, 2 * groups, cols, tokens), BF16),
            pltpu.VMEM((2 * groups, cols, tokens), BF16),
            pltpu.VMEM((tensors, tok_own, kk), F32),
            pltpu.VMEM((tensors - 1, tok_own, kk), F32),
            pltpu.VMEM((tensors, tok_own, kk), BF16),
            pltpu.VMEM((2, 2, groups * cols, kk), F32),
            pltpu.VMEM((2, groups * cols, kk), F32),
            pltpu.VMEM((128, kk), F32),
            pltpu.VMEM((kk // per, per, 128), F32),
            pltpu.VMEM((dps, tensors, per, 128), F32),
            dma((4,)),
            dma((pieces,)), dma((pieces,)),
            dma((pieces,)), dma((pieces,)),
            dma((1 + groups,)), dma((1 + groups,)),
            dma((shifts,)), dma((shifts,)),
            dma((tensors - 1,)), dma((tensors - 1,)),
            dma((tensors - 1,)), dma((tensors - 1,)),
            dma((1,)), dma((1,)),
            dma((dps * tensors - 1,)), dma((dps * tensors - 1,)),
        ],
        compiler_params=pltpu.CompilerParams(
            collective_id=0, has_side_effects=True, vmem_limit_bytes=56 * 1024 * 1024
        ),
    )(
        activations.reshape(tokens, width),
        gradients.reshape(tokens, gwidth),
        basis_in.T,
        basis_out,
    )


def general(activations, gradients, basis_in, basis_out):
    seq_count = lax.axis_size("seq")
    tensor_count = lax.axis_size("tensor")
    replica_count = lax.axis_size("dp")
    seqs_local = activations.shape[0]
    len_local = activations.shape[1]
    width_local = activations.shape[2]
    grad_partial = jnp.einsum(
        "sci,ij->scj",
        gradients,
        lax.all_gather(basis_out, "seq", axis=1, tiled=True),
        preferred_element_type=jnp.float32,
    )
    projected_grad = lax.psum(grad_partial, "tensor").astype(jnp.bfloat16)
    whole_basis = lax.all_gather(basis_in, "seq", axis=1, tiled=True)
    col_total = whole_basis.shape[1]
    per_device = col_total // (seq_count * tensor_count)
    arranged = whole_basis.reshape(width_local, seq_count, tensor_count, per_device)
    group_rows = seq_count * per_device
    product = jnp.einsum(
        "isTj,qci->Tsjqc", arranged, activations, preferred_element_type=jnp.float32
    )
    flat_act = lax.psum_scatter(
        product.reshape(group_rows * lax.axis_size("tensor"), seqs_local * len_local),
        "tensor",
        scatter_dimension=0,
        tiled=True,
    ).astype(jnp.bfloat16)
    projected_act = flat_act.reshape(flat_act.shape[0], seqs_local, len_local)
    partial_blocks = jnp.einsum(
        "rqc,qcj->qrj", projected_act, projected_grad, preferred_element_type=jnp.float32
    )
    blocks = lax.psum_scatter(partial_blocks, "seq", scatter_dimension=1, tiled=True)
    squared = jnp.sum(blocks * blocks, axis=0)
    summed = lax.psum(squared, "dp")
    return summed / (seqs_local * replica_count * len_local * seq_count)


def body(activations, gradients, basis_in, basis_out):
    dps, seqs, tensors = lax.axis_size("dp"), lax.axis_size("seq"), lax.axis_size("tensor")
    s, length, width = activations.shape
    tokens = s * length
    khalf, jhalf = basis_in.shape[1], basis_out.shape[1]
    fits = (
        dps == 2 and seqs == 2 and s == 2 and tensors == 8
        and khalf == 64 and khalf % (8 * tensors) == 0
        and tokens % (16 * tensors) == 0 and tokens % 128 == 0
        and jhalf % 128 == 0 and 2 * jhalf // tensors <= 128 and jhalf >= 256
        and width % (256 * CHUNKS) == 0 and gradients.shape[2] % 32 == 0
        and tokens * width * 2 <= 8 * 1024 * 1024
    )
    return (fused if fits else general)(activations, gradients, basis_in, basis_out)


def solution(mesh):
    return jax.shard_map(
        body,
        mesh=mesh,
        in_specs=(
            P("dp", "seq", "tensor"),
            P("dp", "seq", "tensor"),
            P("tensor", "seq"),
            P("tensor", "seq"),
        ),
        out_specs=P(("seq", "tensor"), None),
        check_vma=False,
    )
```

```python
import functools

import jax
import jax.numpy as jnp
from jax import lax
from jax.experimental import pallas as pl
from jax.experimental.pallas import tpu as pltpu
from jax.sharding import PartitionSpec as P

MESH = pl.DeviceIdType.MESH
F32 = jnp.float32
BF16 = jnp.bfloat16
CHUNKS = 2
SPLIT = 1
DEPTH = 8


def kernel(
    dims,
    act_hbm, grad_hbm, pin_hbm, bout_hbm, out_ref,
    act, grad, pin, bout_own, bout_oth,
    gpart, gmate, gown, gsend, grecv, gfin,
    apart, arecv, afull,
    bpart, brecv, spad, strans, frecv,
    local_sem, ysend, yrecv, xsend, xrecv, msend, mrecv, zsend, zrecv,
    a1send, a1recv, a2send, a2recv, bsend, brecv_sem, fsend, frecv_sem,
):
    dps, seqs, tensors, nz, groups, cols, count = dims
    dp = lax.axis_index("dp")
    y = lax.axis_index("seq")
    t = lax.axis_index("tensor")
    z = t // 2
    c = lax.rem(t, 2)
    oy = 1 - y
    odp = 1 - dp
    mate = z * 2 + (1 - c)
    tokens, width = act.shape
    depth = grad.shape[1]
    per_seq = tokens // 2
    kk = afull.shape[2]

    def remote(src, dst, s, r, to):
        copy = pltpu.make_async_remote_copy(
            src_ref=src, dst_ref=dst, send_sem=s, recv_sem=r,
            device_id=to, device_id_type=MESH,
        )
        copy.start()
        return copy

    loads = []
    for n, (src, dst) in enumerate(
        ((bout_hbm, bout_own), (grad_hbm, grad), (pin_hbm, pin.at[y]), (act_hbm, act))
    ):
        copy = pltpu.make_async_copy(src, dst, local_sem.at[n])
        copy.start()
        loads.append(copy)

    barrier = pltpu.get_barrier_semaphore()
    for ddp in range(dps):
        for d in range(tensors):
            if ddp + d == 0:
                continue
            pl.semaphore_signal(
                barrier, inc=1,
                device_id=(lax.rem(dp + ddp, dps), y, lax.rem(t + d, tensors)),
                device_id_type=MESH,
            )
    pl.semaphore_signal(barrier, inc=1, device_id=(dp, oy, t), device_id_type=MESH)
    pl.semaphore_wait(barrier, dps * tensors)

    pieces = CHUNKS + SPLIT * groups

    def piece(i, own_in, in_slot, own_out):
        if i < CHUNKS:
            size = width // (2 * CHUNKS)
            at = pl.ds(pl.multiple_of((dp * CHUNKS + i) * size, 128), size)
            return own_in.at[:, at] if in_slot is None else own_in.at[in_slot, :, at]
        g, k = divmod(i - CHUNKS, SPLIT)
        size = depth // (2 * SPLIT)
        at = pl.ds(pl.multiple_of((dp * SPLIT + k) * size, 16), size)
        return own_out.at[at, pl.ds(g * 128, 128)]

    ycopies = []
    xcopies = []

    def send_y():
        i = len(ycopies)
        if i < pieces:
            ycopies.append(
                remote(
                    piece(i, pin_hbm, None, bout_hbm), piece(i, pin, y, bout_oth),
                    ysend.at[i], yrecv.at[i], (dp, oy, t),
                )
            )

    def forward():
        i = len(xcopies)
        ycopies[i].wait_recv()
        send_y()
        ref = piece(i, pin, oy, bout_oth)
        xcopies.append(remote(ref, ref, xsend.at[i], xrecv.at[i], (odp, y, t)))

    mates = []

    def project_grad(basis, first, number):
        n = len(mates)
        total = lax.dot_general(
            basis, grad[...], (((0,), (1,)), ((), ())), preferred_element_type=F32
        )
        gpart[first : first + number] = total.reshape(number, 2, nz, cols, tokens)
        part = pl.ds(first, number)
        mates.append(
            remote(
                gpart.at[part, 1 - c], gmate.at[part], msend.at[n], mrecv.at[n],
                (dp, y, mate),
            )
        )

    zcopies = []

    def scatter_grad(n, first, number):
        mates[n].wait_recv()
        part = pl.ds(first, number)
        gsend[part] = (gpart[part, c] + gmate[part]).astype(BF16)
        gown[part] = gpart[part, c, z] + gmate[part, z]
        copies = []
        for d in range(1, nz):
            oz = lax.rem(z + d, nz)
            i = n * (nz - 1) + d - 1
            copies.append(
                remote(
                    gsend.at[part, oz], grecv.at[d - 1, part], zsend.at[i], zrecv.at[i],
                    (dp, y, oz * 2 + c),
                )
            )
        zcopies.append(copies)

    def finish_grad(n, first, number):
        part = pl.ds(first, number)
        total = gown[part]
        for d in range(1, nz):
            zcopies[n][d - 1].wait_recv()
            total = total + grecv[d - 1, part].astype(F32)
        gfin[part] = total.astype(BF16)

    def project_act(half):
        at = pl.ds(pl.multiple_of(half * (width // 2), 128), width // 2)
        basis = pin[:, :, at].reshape(kk, width // 2)
        return lax.dot_general(
            act[:, at], basis, (((1,), (1,)), ((), ())), preferred_element_type=F32
        )

    def outer(slot, masked0, masked1):
        at = jnp.where(y == slot, 0, 1)
        part = gfin[slot * groups : (slot + 1) * groups].reshape(groups * cols, tokens)
        bpart[0, at] = jnp.dot(part, masked0, preferred_element_type=F32)
        bpart[1, at] = jnp.dot(part, masked1, preferred_element_type=F32)

    for _ in range(DEPTH):
        send_y()
    loads[0].wait()
    loads[1].wait()
    project_grad(bout_own[...], 0, groups)
    loads[2].wait()
    loads[3].wait()
    for _ in range(CHUNKS):
        forward()
    apart[...] = project_act(dp).reshape(apart.shape)
    scatter_grad(0, 0, groups)
    for _ in range(SPLIT):
        forward()
    for i in range(CHUNKS):
        xcopies[i].wait_recv()
    apart[...] = apart[...] + project_act(odp).reshape(apart.shape)
    a1 = []
    for d in range(1, tensors):
        ot = lax.rem(t + d, tensors)
        a1.append(
            remote(apart.at[ot], arecv.at[d - 1], a1send.at[d - 1], a1recv.at[d - 1], (dp, y, ot))
        )
    a2 = []
    for g in range(groups):
        if g + 1 < groups:
            for _ in range(SPLIT):
                forward()
        if g == 1:
            total = apart[t]
            for d in range(1, tensors):
                a1[d - 1].wait_recv()
                total = total + arecv[d - 1]
            afull[t] = total.astype(BF16)
            for d in range(1, tensors):
                ot = lax.rem(t + d, tensors)
                a2.append(
                    remote(
                        afull.at[t], afull.at[t], a2send.at[d - 1], a2recv.at[d - 1],
                        (dp, y, ot),
                    )
                )
        if g == groups - 1:
            finish_grad(0, 0, groups)
        for k in range(SPLIT):
            xcopies[CHUNKS + g * SPLIT + k].wait_recv()
        project_grad(bout_oth[:, g * 128 : (g + 1) * 128], groups + g, 1)
        if g > 0:
            scatter_grad(g, groups + g - 1, 1)
    for copy in a2:
        copy.wait_recv()
    whole = afull[...].astype(F32).reshape(tokens, kk)
    turned = pltpu.roll(whole, kk // 2, 1)
    lane = lax.broadcasted_iota(jnp.int32, (tokens, kk), 1)
    row = lax.broadcasted_iota(jnp.int32, (tokens, kk), 0)
    low = lane < kk // 2
    mine = (row < per_seq) == low
    masked0 = jnp.where(mine, jnp.where(low, whole, turned), 0.0).astype(BF16)
    masked1 = jnp.where(mine, jnp.where(low, turned, whole), 0.0).astype(BF16)
    scatter_grad(groups, 2 * groups - 1, 1)
    outer(0, masked0, masked1)
    bcopies = [
        remote(bpart.at[oy, y], brecv.at[y], bsend.at[0], brecv_sem.at[0], (dp, oy, t))
    ]
    spad[...] = jnp.zeros_like(spad)
    for g in range(groups):
        finish_grad(1 + g, groups + g, 1)
    outer(1, masked0, masked1)
    bcopies.append(
        remote(bpart.at[oy, oy], brecv.at[oy], bsend.at[1], brecv_sem.at[1], (dp, oy, t))
    )
    zall = [copy for copies in zcopies for copy in copies]
    for copy in ycopies + xcopies + mates + zall + a1 + a2:
        copy.wait_send()
    for copy in bcopies:
        copy.wait_recv()
    both = (bpart[y] + brecv[...]).reshape(2 * groups * cols, kk)
    square = both * both
    spad[pl.ds(0, 2 * groups * cols), :] = square + pltpu.roll(square, kk // 2, 1)
    strans[...] = spad[...].T.reshape(strans.shape)
    place = c * nz + z
    frecv[0, place] = strans[t]
    fcopies = []
    for ddp in range(dps):
        for d in range(tensors):
            if ddp + d == 0:
                continue
            i = ddp * tensors + d - 1
            ot = lax.rem(t + d, tensors)
            fcopies.append(
                remote(
                    strans.at[ot], frecv.at[ddp, place], fsend.at[i], frecv_sem.at[i],
                    (lax.rem(dp + ddp, dps), y, ot),
                )
            )
    for copy in fcopies:
        copy.wait_recv()
    total = frecv[0] + frecv[1]
    lane = lax.broadcasted_iota(jnp.int32, total.shape[1:], 1)
    for block in range(2 * groups):
        found = jnp.zeros(total.shape[1:], F32)
        for p in range(tensors):
            shift = ((p - block) * cols) % 128
            moved = pltpu.roll(total[p], shift, 1) if shift else total[p]
            found = jnp.where(lane // cols == p, moved, found)
        out_ref[:, block * 128 : (block + 1) * 128] = found
    for copy in bcopies + fcopies:
        copy.wait_send()


def fused(activations, gradients, basis_in, basis_out):
    dps, seqs, tensors = lax.axis_size("dp"), lax.axis_size("seq"), lax.axis_size("tensor")
    s, length, width = activations.shape
    gwidth = gradients.shape[2]
    tokens = s * length
    nz = tensors // 2
    khalf = basis_in.shape[1]
    jhalf = basis_out.shape[1]
    kk = 2 * khalf
    groups = jhalf // 128
    cols = 128 // tensors
    per = khalf // tensors
    count = s * dps * length * seqs
    dma = pltpu.SemaphoreType.DMA
    tok_own = tokens // tensors
    pieces = CHUNKS + SPLIT * groups
    shifts = (1 + groups) * (nz - 1)
    total = pl.pallas_call(
        functools.partial(kernel, (dps, seqs, tensors, nz, groups, cols, count)),
        out_shape=jax.ShapeDtypeStruct((per, 2 * jhalf), F32),
        in_specs=[pl.BlockSpec(memory_space=pltpu.HBM)] * 4,
        out_specs=pl.BlockSpec(memory_space=pltpu.VMEM),
        scratch_shapes=[
            pltpu.VMEM((tokens, width), BF16),
            pltpu.VMEM((tokens, gwidth), BF16),
            pltpu.VMEM((2, khalf, width), BF16),
            pltpu.VMEM((gwidth, jhalf), BF16),
            pltpu.VMEM((gwidth, jhalf), BF16),
            pltpu.VMEM((2 * groups, 2, nz, cols, tokens), F32),
            pltpu.VMEM((2 * groups, nz, cols, tokens), F32),
            pltpu.VMEM((2 * groups, cols, tokens), F32),
            pltpu.VMEM((2 * groups, nz, cols, tokens), BF16),
            pltpu.VMEM((nz - 1, 2 * groups, cols, tokens), BF16),
            pltpu.VMEM((2 * groups, cols, tokens), BF16),
            pltpu.VMEM((tensors, tok_own, kk), F32),
            pltpu.VMEM((tensors - 1, tok_own, kk), F32),
            pltpu.VMEM((tensors, tok_own, kk), BF16),
            pltpu.VMEM((2, 2, groups * cols, kk), F32),
            pltpu.VMEM((2, groups * cols, kk), F32),
            pltpu.VMEM((128, kk), F32),
            pltpu.VMEM((kk // per, per, 128), F32),
            pltpu.VMEM((dps, tensors, per, 128), F32),
            dma((4,)),
            dma((pieces,)), dma((pieces,)),
            dma((pieces,)), dma((pieces,)),
            dma((1 + groups,)), dma((1 + groups,)),
            dma((shifts,)), dma((shifts,)),
            dma((tensors - 1,)), dma((tensors - 1,)),
            dma((tensors - 1,)), dma((tensors - 1,)),
            dma((2,)), dma((2,)),
            dma((dps * tensors - 1,)), dma((dps * tensors - 1,)),
        ],
        compiler_params=pltpu.CompilerParams(
            collective_id=0, has_side_effects=True, vmem_limit_bytes=56 * 1024 * 1024
        ),
    )(
        activations.reshape(tokens, width),
        gradients.reshape(tokens, gwidth),
        basis_in.T,
        basis_out,
    )
    return total / count


def general(activations, gradients, basis_in, basis_out):
    seq_count = lax.axis_size("seq")
    tensor_count = lax.axis_size("tensor")
    replica_count = lax.axis_size("dp")
    seqs_local = activations.shape[0]
    len_local = activations.shape[1]
    width_local = activations.shape[2]
    grad_partial = jnp.einsum(
        "sci,ij->scj",
        gradients,
        lax.all_gather(basis_out, "seq", axis=1, tiled=True),
        preferred_element_type=jnp.float32,
    )
    projected_grad = lax.psum(grad_partial, "tensor").astype(jnp.bfloat16)
    whole_basis = lax.all_gather(basis_in, "seq", axis=1, tiled=True)
    col_total = whole_basis.shape[1]
    per_device = col_total // (seq_count * tensor_count)
    arranged = whole_basis.reshape(width_local, seq_count, tensor_count, per_device)
    group_rows = seq_count * per_device
    product = jnp.einsum(
        "isTj,qci->Tsjqc", arranged, activations, preferred_element_type=jnp.float32
    )
    flat_act = lax.psum_scatter(
        product.reshape(group_rows * lax.axis_size("tensor"), seqs_local * len_local),
        "tensor",
        scatter_dimension=0,
        tiled=True,
    ).astype(jnp.bfloat16)
    projected_act = flat_act.reshape(flat_act.shape[0], seqs_local, len_local)
    partial_blocks = jnp.einsum(
        "rqc,qcj->qrj", projected_act, projected_grad, preferred_element_type=jnp.float32
    )
    blocks = lax.psum_scatter(partial_blocks, "seq", scatter_dimension=1, tiled=True)
    squared = jnp.sum(blocks * blocks, axis=0)
    summed = lax.psum(squared, "dp")
    return summed / (seqs_local * replica_count * len_local * seq_count)


def body(activations, gradients, basis_in, basis_out):
    dps, seqs, tensors = lax.axis_size("dp"), lax.axis_size("seq"), lax.axis_size("tensor")
    s, length, width = activations.shape
    tokens = s * length
    khalf, jhalf = basis_in.shape[1], basis_out.shape[1]
    fits = (
        dps == 2 and seqs == 2 and s == 2 and tensors == 8
        and khalf == 64 and khalf % (8 * tensors) == 0
        and tokens % (16 * tensors) == 0 and tokens % 128 == 0
        and jhalf % 128 == 0 and 2 * jhalf // tensors <= 128 and jhalf >= 256
        and width % (256 * CHUNKS) == 0 and gradients.shape[2] % (32 * SPLIT) == 0
        and tokens * width * 2 <= 8 * 1024 * 1024
    )
    return (fused if fits else general)(activations, gradients, basis_in, basis_out)


def solution(mesh):
    return jax.shard_map(
        body,
        mesh=mesh,
        in_specs=(
            P("dp", "seq", "tensor"),
            P("dp", "seq", "tensor"),
            P("tensor", "seq"),
            P("tensor", "seq"),
        ),
        out_specs=P(("seq", "tensor"), None),
        check_vma=False,
    )
```
